32 devices in a mesh: groups: 2 (over y), tok: 8 (over z, x), voc: 2 (over core).
Axes of the slice: x: 2, y: 2, z: 4, core: 2. Of those that a mesh axis runs over, the one named last changes fastest.
Arguments:
- teacher: bfloat16 [16, 48, 81920], P(('groups', 'tok'), None, 'voc'), parts along dimension 0, may hold values from 0.0009994507 to 1
- student: bfloat16 [48, 16, 65536], P('voc', 'groups', 'tok'), parts along dimension 1, may hold values from -8 to 284
- block_maps: bfloat16 [512, 2, 4, 128, 128], P('tok', 'voc'), may hold values from 0.0009994507 to 1
- slot_index: int32 [512, 2, 4], P('tok', 'voc'), may hold values from 0 to 39, as said below
- slot_count: int32 [512, 2], P('tok', 'voc'), may hold values from 0 to 4, as said below
Outputs:
- logit_grad: bfloat16 [48, 16, 65536], P('voc', 'groups', 'tok'), parts along dimension 1
- divergence: float32 [48, 16], P('voc', 'groups'), parts along dimension 1
The draws below stay inside these ranges and needn't reach their ends.
There are 2 independent parts, one for each index of `groups`. The reference program is written for one: setup_inputs(seed, part) draws one part's arguments, and reference() takes and returns one part's arrays. A program takes and returns all parts, laid end to end along the dimension named above; an argument that names none is the same for every part. Nothing has to cross between parts.
Inputs may be any that keep to these rules, and one draw needn't show every extreme that they name: `slot_index`: within one student block and half the 4 indices are distinct. slot_count[s, 0] is at least 1 for every student block s.
All inputs are finite; a program needn't handle non-finite values.
Results may differ from the reference program's by a relative error of at most 0.0055.
Values may be sent and summed in bfloat16 or wider, within the bound.
A program may use at most 128 MiB of HBM per device.

```python
import math
import jax
import jax.numpy as jnp
from jax import lax

BLK = 128
TB = 640
SB = 512
KH = 4
TOK_DEV = 48
VT = 81920
VS = 65536
SHARDS = 8
N_TOK = 8


def draw_student(key, part):
    key = jax.random.fold_in(key, 13)
    first_key = jax.random.fold_in(key, 0)
    values = jnp.clip(2.0 * jax.random.normal(first_key, (TOK_DEV, SHARDS, VS), jnp.float32), -8.0, 8.0)
    return values.astype(jnp.bfloat16)


def draw_slot_index(key, part):
    key = jax.random.fold_in(key, 11)
    span_blocks = TB // (2 * N_TOK)
    scores = jax.random.randint(key, (SB, 2, span_blocks), 0, 1 << 20) * span_blocks
    scores = scores + jnp.arange(span_blocks, dtype=jnp.int32)
    order = jnp.argsort(scores, axis=-1, stable=True)
    return order[:, :, :KH].astype(jnp.int32)


def draw_slot_count(key, part):
    key = jax.random.fold_in(key, 12)
    first_key, second_key = jax.random.split(key)
    lower_count = jax.random.randint(first_key, (SB, 1), 1, KH + 1)
    upper_count = jax.random.randint(second_key, (SB, 1), 0, KH + 1)
    return jnp.concatenate([lower_count, upper_count], axis=1).astype(jnp.int32)


def block_levels(key, extent, cuts, least, largest):
    loudness, own = 1.0, jax.random.fold_in(key, 6)
    for axis_at, blocks in cuts:
        heights = jnp.exp(jax.random.uniform(jax.random.fold_in(own, axis_at), (blocks,), jnp.float32, least / len(cuts), largest / len(cuts)))
        loudness = loudness * jnp.repeat(heights, extent[axis_at] // blocks).reshape([-1 if axis == axis_at else 1 for axis in range(len(extent))])
    return loudness


def setup_inputs(seed: int = 0, part: int = 0) -> dict:
    arg_keys = jax.random.split(jax.random.key(seed), 6)
    own_keys = jax.random.split(jax.random.fold_in(arg_keys[5], part), 6)
    teacher = jnp.clip(jnp.exp(math.log(1.0) - 6.9083047 * jax.random.uniform(own_keys[0], (SHARDS, TOK_DEV, VT), jnp.float32) ** block_levels(own_keys[0], (SHARDS, TOK_DEV, VT), ((0, 8), (2, 2)), -0.2, 0.2)), 0.0009994507, 1.0).astype(jnp.bfloat16)
    student = draw_student(jax.random.fold_in(jax.random.fold_in(arg_keys[5], part), 71), part)
    block_maps = jnp.clip(jnp.exp(math.log(1.0) - 6.9083047 * jax.random.uniform(arg_keys[2], (SB, 2, KH, BLK, BLK), jnp.float32) ** block_levels(arg_keys[2], (SB, 2, KH, BLK, BLK), ((0, 8), (1, 2)), -0.2, 0.2)), 0.0009994507, 1.0).astype(jnp.bfloat16)
    slot_index = draw_slot_index(jax.random.fold_in(arg_keys[5], 71), part)
    slot_count = draw_slot_count(jax.random.fold_in(arg_keys[5], 71), part)
    return dict(teacher=teacher, student=student, block_maps=block_maps, slot_index=slot_index, slot_count=slot_count)


def apply_maps(columns, matrices, indices, counts, span_blocks):
    slots_all = matrices.shape[1]
    blocks = matrices.shape[-1]
    student_blocks = matrices.shape[0]
    active = (jnp.arange(slots_all, dtype=jnp.int32)[None, :] < counts[:, None]).astype(jnp.float32)
    onehot = (indices[:, :, None] == jnp.arange(span_blocks, dtype=jnp.int32)[None, None, :]).astype(jnp.float32)
    onehot = (onehot * active[:, :, None]).astype(jnp.bfloat16)
    lead = columns.shape[:-1]
    split_cols = columns.reshape(lead + (span_blocks, blocks))
    picked = jnp.einsum("...ta,skt->...ska", split_cols, onehot, preferred_element_type=jnp.float32).astype(jnp.bfloat16)
    result = jnp.einsum("...ska,skab->...sb", picked, matrices, preferred_element_type=jnp.float32)
    return result.reshape(lead + (student_blocks * blocks,))


def reference(teacher, student, block_maps, slot_index, slot_count):
    row_major = jnp.swapaxes(teacher, 0, 1)
    group_blocks = TB // (2 * N_TOK)
    group_students = SB // N_TOK
    half_width = TB * BLK // 2
    span = group_blocks * BLK

    def one_group(group_idx):
        group_idx = group_idx.astype(jnp.int32)
        lower_cols = lax.dynamic_slice_in_dim(row_major, group_idx * span, span, 2)
        upper_cols = lax.dynamic_slice_in_dim(row_major, half_width + group_idx * span, span, 2)
        first_block = group_idx * group_students
        matrices = lax.dynamic_slice_in_dim(block_maps, first_block, group_students, 0)
        indices = lax.dynamic_slice_in_dim(slot_index, first_block, group_students, 0)
        counts = lax.dynamic_slice_in_dim(slot_count, first_block, group_students, 0)
        summands = []
        for which, columns in ((0, lower_cols), (1, upper_cols)):
            rounded = apply_maps(columns, matrices[:, which], indices[:, which], counts[:, which], group_blocks).astype(jnp.bfloat16)
            summands.append(lax.optimization_barrier(rounded).astype(jnp.float32))
        return summands[0] + summands[1]

    mapped = lax.map(one_group, jnp.arange(N_TOK, dtype=jnp.int32))
    mapped = jnp.moveaxis(mapped, 0, 2).reshape(TOK_DEV, N_TOK, SB * BLK)
    logit_f = student.astype(jnp.float32)
    row_top = jnp.max(logit_f, axis=-1)
    shifted = jnp.exp(logit_f - row_top[..., None])
    exp_total = jnp.sum(shifted, axis=-1)
    mass = jnp.sum(mapped, axis=-1)
    entropy_part = jnp.sum(mapped * jnp.log(mapped), axis=-1)
    cross_part = jnp.sum(mapped * logit_f, axis=-1)
    divergence = entropy_part / mass - jnp.log(mass) - cross_part / mass + row_top + jnp.log(exp_total)
    logit_grad = (VS * (shifted / exp_total[..., None] - mapped / mass[..., None])).astype(jnp.bfloat16)
    return logit_grad, divergence
```

```python
import functools

import jax
import jax.numpy as jnp
from jax import lax
from jax.experimental import pallas as pl
from jax.experimental.pallas import tpu as pltpu
from jax.sharding import PartitionSpec as P

MESH = pl.DeviceIdType.MESH
LANES = 128
FIELDS = 8
WINDOW = 3


def kernel(
    n, words, teacher, student_hbm, maps_hbm, slots, grad, div,
    cols, work, maps, student, part, other_part, stats, gathered,
    local_sem, send_sem, recv_sem, half_send, half_recv, stat_send, stat_recv,
):
    rows = cols.shape[1]
    span = cols.shape[2]
    teacher_blocks = span // LANES
    student_blocks = maps.shape[0]
    slots_all = maps.shape[1] // LANES
    half_rows = student.shape[1]
    width = student.shape[2]
    lanes = stats.shape[1]
    chunk = 512
    me = lax.axis_index("tok")
    voc = lax.axis_index("voc")
    other = 1 - voc

    def shift_of(step):
        near = (step + 1) // 2
        return n // 2 + (1 - 2 * lax.rem(step, 2)) * near

    def column_copy(step):
        target = lax.rem(me + shift_of(step), n)
        return pltpu.make_async_remote_copy(
            src_ref=teacher.at[:, pl.ds(pl.multiple_of(target * span, LANES), span)],
            dst_ref=cols.at[step + 1],
            send_sem=send_sem.at[step],
            recv_sem=recv_sem.at[step],
            device_id={"tok": target},
            device_id_type=MESH,
        )

    def half_copy(source):
        return pltpu.make_async_remote_copy(
            src_ref=part.at[source, pl.ds(pl.multiple_of(other * half_rows, 8), half_rows)],
            dst_ref=other_part.at[source],
            send_sem=half_send.at[source],
            recv_sem=half_recv.at[source],
            device_id={"voc": other},
            device_id_type=MESH,
        )

    def stat_copy(step):
        target = lax.rem(me + step + 1, n)
        return pltpu.make_async_remote_copy(
            src_ref=stats,
            dst_ref=gathered.at[step],
            send_sem=stat_send.at[step],
            recv_sem=stat_recv.at[step],
            device_id={"tok": target},
            device_id_type=MESH,
        )

    own_copy = pltpu.make_async_copy(
        teacher.at[:, pl.ds(pl.multiple_of(me * span, LANES), span)], cols.at[0], local_sem.at[0]
    )
    maps_copy = pltpu.make_async_copy(maps_hbm, maps, local_sem.at[1])
    student_copy = pltpu.make_async_copy(student_hbm, student, local_sem.at[2])
    own_copy.start()
    maps_copy.start()
    student_copy.start()

    barrier = pltpu.get_barrier_semaphore()

    @pl.loop(1, n)
    def _(step):
        pl.semaphore_signal(
            barrier, inc=1, device_id={"tok": lax.rem(me + step, n)}, device_id_type=MESH
        )

    pl.semaphore_signal(barrier, inc=1, device_id={"voc": other}, device_id_type=MESH)
    pl.semaphore_wait(barrier, n)

    for step in range(min(WINDOW, n - 1)):
        column_copy(step).start()

    work[teacher_blocks] = jnp.zeros((rows, LANES), work.dtype)
    stats[...] = jnp.zeros_like(stats)
    lane = lax.broadcasted_iota(jnp.int32, (half_rows, lanes), 1)

    def map_rows(slot, source):
        for block in range(teacher_blocks):
            work[block] = cols[slot, :, block * LANES : (block + 1) * LANES]

        @pl.loop(0, student_blocks, unroll=4)
        def _(block):
            picked = jnp.concatenate(
                [work[slots[block * slots_all + k]] for k in range(slots_all)], axis=1
            )
            part[source, :, pl.ds(pl.multiple_of(block * LANES, LANES), LANES)] = jnp.dot(
                picked, maps[block], preferred_element_type=jnp.float32
            )

        half_copy(source).start()

    def fold(x):
        return functools.reduce(
            lambda a, b: a + b, [x[:, c : c + LANES] for c in range(0, chunk, LANES)]
        )

    def mapped_of(source, at):
        mine = part[source, pl.ds(pl.multiple_of(voc * half_rows, 8), half_rows), at]
        return mine + other_part[source, :, at]

    def row_stats(source):
        def top_step(c, top):
            at = pl.ds(pl.multiple_of(c * chunk, chunk), chunk)
            x = student[source, :, at].astype(jnp.float32)
            for k in range(0, chunk, LANES):
                top = jnp.maximum(top, x[:, k : k + LANES])
            return top

        start = jnp.full((half_rows, LANES), -jnp.inf, jnp.float32)
        top = jnp.max(
            lax.fori_loop(0, width // chunk, top_step, start), axis=1, keepdims=True
        )
        half_copy(source).wait()

        def sum_step(c, sums):
            at = pl.ds(pl.multiple_of(c * chunk, chunk), chunk)
            x = student[source, :, at].astype(jnp.float32)
            mapped = mapped_of(source, at)
            terms = (jnp.exp(x - top), mapped, mapped * jnp.log(mapped), mapped * x)
            return tuple(s + fold(t) for s, t in zip(sums, terms))

        zero = jnp.zeros((half_rows, LANES), jnp.float32)
        sums = lax.fori_loop(0, width // chunk, sum_step, (zero,) * 4)
        packed = stats[...]
        values = (top,) + tuple(jnp.sum(s, axis=1, keepdims=True) for s in sums)
        for field, value in enumerate(values):
            packed = jnp.where(lane == source * FIELDS + field, value, packed)
        stats[...] = packed

    own_copy.wait()
    maps_copy.wait()
    map_rows(0, me)
    student_copy.wait()

    def source_of(step):
        return lax.rem(me - shift_of(step) + n, n)

    @pl.loop(0, n - 1)
    def _(step):
        column_copy(step).wait()

        @pl.when(step + WINDOW < n - 1)
        def _():
            column_copy(step + WINDOW).start()

        map_rows(step + 1, source_of(step))
        row_stats(lax.select(step == 0, me, source_of(jnp.maximum(step - 1, 0))))

    row_stats(source_of(n - 2))

    @pl.loop(0, n - 1)
    def _(step):
        stat_copy(step).start()

    @pl.loop(0, n - 1)
    def _(step):
        stat_copy(step).wait()

    own = stats[...]
    top = lax.fori_loop(0, n - 1, lambda d, t: jnp.maximum(t, gathered[d]), own)
    is_exp = lax.rem(lane, FIELDS) == 1

    def scaled(g):
        return jnp.where(is_exp, g * jnp.exp(pltpu.roll(g - top, 1, 1)), g)

    total = lax.fori_loop(0, n - 1, lambda d, t: t + scaled(gathered[d]), scaled(own))
    exp_total, mass, entropy, cross = (pltpu.roll(total, lanes - k, 1) for k in (1, 2, 3, 4))
    div[...] = entropy / mass - jnp.log(mass) - cross / mass + top + jnp.log(exp_total)
    exp_scale = words / exp_total
    map_scale = words / mass

    @pl.loop(0, n)
    def _(source):
        here = lane == source * FIELDS
        row_top, row_exp, row_map = (
            jnp.sum(jnp.where(here, v, 0.0), axis=1, keepdims=True)
            for v in (top, exp_scale, map_scale)
        )

        @pl.loop(0, width // chunk)
        def _(c):
            at = pl.ds(pl.multiple_of(c * chunk, chunk), chunk)
            x = student[source, :, at].astype(jnp.float32)
            value = jnp.exp(x - row_top) * row_exp - mapped_of(source, at) * row_map
            grad[source, :, at] = value.astype(grad.dtype)


def body(teacher, student, block_maps, slot_index, slot_count):
    n = lax.axis_size("tok")
    rows = teacher.shape[1]
    half_rows, _, width = student.shape
    student_blocks, _, slots_all, depth, block = block_maps.shape
    span = teacher.shape[2] // n
    teacher_blocks = span // block
    lanes = max(LANES, n * FIELDS)
    used = jnp.arange(slots_all, dtype=jnp.int32)[None, :] < slot_count[:, :1]
    slots = jnp.where(used, slot_index[:, 0], teacher_blocks).reshape(-1)
    anywhere = pl.BlockSpec(memory_space=pl.ANY)
    in_vmem = pl.BlockSpec(memory_space=pltpu.VMEM)
    dma = pltpu.SemaphoreType.DMA
    grad, div = pl.pallas_call(
        functools.partial(kernel, n, float(n * width)),
        out_shape=(
            jax.ShapeDtypeStruct((n, half_rows, width), jnp.bfloat16),
            jax.ShapeDtypeStruct((half_rows, lanes), jnp.float32),
        ),
        in_specs=[anywhere, anywhere, anywhere, pl.BlockSpec(memory_space=pltpu.SMEM)],
        out_specs=(in_vmem, in_vmem),
        scratch_shapes=[
            pltpu.VMEM((n, rows, span), jnp.bfloat16),
            pltpu.VMEM((teacher_blocks + 1, rows, block), jnp.bfloat16),
            pltpu.VMEM((student_blocks, slots_all * depth, block), jnp.bfloat16),
            pltpu.VMEM((n, half_rows, width), jnp.bfloat16),
            pltpu.VMEM((n, rows, width), jnp.float32),
            pltpu.VMEM((n, half_rows, width), jnp.float32),
            pltpu.VMEM((half_rows, lanes), jnp.float32),
            pltpu.VMEM((n - 1, half_rows, lanes), jnp.float32),
            dma((3,)),
            dma((n - 1,)),
            dma((n - 1,)),
            dma((n,)),
            dma((n,)),
            dma((n - 1,)),
            dma((n - 1,)),
        ],
        compiler_params=pltpu.CompilerParams(
            collective_id=0, has_side_effects=True, vmem_limit_bytes=56 * 2**20
        ),
    )(
        teacher[0],
        jnp.swapaxes(student, 0, 1),
        block_maps.reshape(student_blocks, slots_all * depth, block),
        slots,
    )
    divergence = div.reshape(half_rows, -1, FIELDS)[:, :n, 0]
    return jnp.swapaxes(grad, 0, 1), divergence


def solution(mesh):
    return jax.shard_map(
        body,
        mesh=mesh,
        in_specs=(
            P(("groups", "tok"), None, "voc"),
            P("voc", "groups", "tok"),
            P("tok", "voc", None, None, None),
            P("tok", "voc", None),
            P("tok", "voc"),
        ),
        out_specs=(P("voc", "groups", "tok"), P("voc", "groups")),
        check_vma=False,
    )
```

```python
import functools

import jax
import jax.numpy as jnp
from jax import lax
from jax.experimental import pallas as pl
from jax.experimental.pallas import tpu as pltpu
from jax.sharding import PartitionSpec as P

MESH = pl.DeviceIdType.MESH
LANES = 128
FIELDS = 8
WINDOW = 4


def kernel(
    n, words, teacher, student_hbm, maps_hbm, slots, grad, div,
    cols, work, maps, student, part, other_part, stats, gathered,
    local_sem, send_sem, recv_sem, half_send, half_recv, stat_send, stat_recv,
):
    rows = cols.shape[1]
    span = cols.shape[2]
    teacher_blocks = span // LANES
    student_blocks = maps.shape[0]
    slots_all = maps.shape[1] // LANES
    half_rows = student.shape[1]
    width = student.shape[2]
    lanes = stats.shape[1]
    chunk = 512
    me = lax.axis_index("tok")
    voc = lax.axis_index("voc")
    other = 1 - voc

    def partner(step):
        half = (step + 1) // 2
        odd = lax.rem(step, 2)
        mask = odd * half + (1 - odd) * (n - 1 - half)
        total, bit = 0, 1
        while bit < n:
            mine = lax.rem(me // bit, 2)
            flip = lax.rem(mask // bit, 2)
            total = total + bit * (mine + flip - 2 * mine * flip)
            bit *= 2
        return total

    def column_copy(step):
        target = partner(step)
        return pltpu.make_async_remote_copy(
            src_ref=teacher.at[:, pl.ds(pl.multiple_of(target * span, LANES), span)],
            dst_ref=cols.at[step + 1],
            send_sem=send_sem.at[step],
            recv_sem=recv_sem.at[step],
            device_id={"tok": target},
            device_id_type=MESH,
        )

    def half_copy(source):
        return pltpu.make_async_remote_copy(
            src_ref=part.at[source, pl.ds(pl.multiple_of(other * half_rows, 8), half_rows)],
            dst_ref=other_part.at[source],
            send_sem=half_send.at[source],
            recv_sem=half_recv.at[source],
            device_id={"voc": other},
            device_id_type=MESH,
        )

    def stat_copy(step):
        target = lax.rem(me + step + 1, n)
        return pltpu.make_async_remote_copy(
            src_ref=stats,
            dst_ref=gathered.at[step],
            send_sem=stat_send.at[step],
            recv_sem=stat_recv.at[step],
            device_id={"tok": target},
            device_id_type=MESH,
        )

    own_copy = pltpu.make_async_copy(
        teacher.at[:, pl.ds(pl.multiple_of(me * span, LANES), span)], cols.at[0], local_sem.at[0]
    )
    maps_copy = pltpu.make_async_copy(maps_hbm, maps, local_sem.at[1])
    student_copy = pltpu.make_async_copy(student_hbm, student, local_sem.at[2])
    own_copy.start()
    maps_copy.start()
    student_copy.start()

    barrier = pltpu.get_barrier_semaphore()

    @pl.loop(1, n)
    def _(step):
        pl.semaphore_signal(
            barrier, inc=1, device_id={"tok": lax.rem(me + step, n)}, device_id_type=MESH
        )

    pl.semaphore_signal(barrier, inc=1, device_id={"voc": other}, device_id_type=MESH)
    pl.semaphore_wait(barrier, n)

    for step in range(min(WINDOW, n - 1)):
        column_copy(step).start()

    work[teacher_blocks] = jnp.zeros((rows, LANES), work.dtype)
    stats[...] = jnp.zeros_like(stats)
    lane = lax.broadcasted_iota(jnp.int32, (half_rows, lanes), 1)

    def map_rows(slot, source):
        for block in range(teacher_blocks):
            work[block] = cols[slot, :, block * LANES : (block + 1) * LANES]

        @pl.loop(0, student_blocks, unroll=4)
        def _(block):
            picked = jnp.concatenate(
                [work[slots[block * slots_all + k]] for k in range(slots_all)], axis=1
            )
            part[source, :, pl.ds(pl.multiple_of(block * LANES, LANES), LANES)] = jnp.dot(
                picked, maps[block], preferred_element_type=jnp.float32
            )

        half_copy(source).start()

    def fold(x):
        return functools.reduce(
            lambda a, b: a + b, [x[:, c : c + LANES] for c in range(0, chunk, LANES)]
        )

    def mapped_of(source, at):
        mine = part[source, pl.ds(pl.multiple_of(voc * half_rows, 8), half_rows), at]
        return mine + other_part[source, :, at]

    def row_stats(source):
        def top_step(c, top):
            at = pl.ds(pl.multiple_of(c * chunk, chunk), chunk)
            x = student[source, :, at].astype(jnp.float32)
            for k in range(0, chunk, LANES):
                top = jnp.maximum(top, x[:, k : k + LANES])
            return top

        start = jnp.full((half_rows, LANES), -jnp.inf, jnp.float32)
        top = jnp.max(
            lax.fori_loop(0, width // chunk, top_step, start), axis=1, keepdims=True
        )
        half_copy(source).wait()

        def sum_step(c, sums):
            at = pl.ds(pl.multiple_of(c * chunk, chunk), chunk)
            x = student[source, :, at].astype(jnp.float32)
            mapped = mapped_of(source, at)
            terms = (jnp.exp(x - top), mapped, mapped * jnp.log(mapped), mapped * x)
            return tuple(s + fold(t) for s, t in zip(sums, terms))

        zero = jnp.zeros((half_rows, LANES), jnp.float32)
        sums = lax.fori_loop(0, width // chunk, sum_step, (zero,) * 4)
        packed = stats[...]
        values = (top,) + tuple(jnp.sum(s, axis=1, keepdims=True) for s in sums)
        for field, value in enumerate(values):
            packed = jnp.where(lane == source * FIELDS + field, value, packed)
        stats[...] = packed

    own_copy.wait()
    maps_copy.wait()
    map_rows(0, me)
    student_copy.wait()

    def source_of(step):
        return partner(step)

    @pl.loop(0, n - 1)
    def _(step):
        column_copy(step).wait()

        @pl.when(step + WINDOW < n - 1)
        def _():
            column_copy(step + WINDOW).start()

        map_rows(step + 1, source_of(step))
        row_stats(lax.select(step == 0, me, source_of(jnp.maximum(step - 1, 0))))

    row_stats(source_of(n - 2))

    @pl.loop(0, n - 1)
    def _(step):
        stat_copy(step).start()

    @pl.loop(0, n - 1)
    def _(step):
        stat_copy(step).wait()

    own = stats[...]
    top = lax.fori_loop(0, n - 1, lambda d, t: jnp.maximum(t, gathered[d]), own)
    is_exp = lax.rem(lane, FIELDS) == 1

    def scaled(g):
        return jnp.where(is_exp, g * jnp.exp(pltpu.roll(g - top, 1, 1)), g)

    total = lax.fori_loop(0, n - 1, lambda d, t: t + scaled(gathered[d]), scaled(own))
    exp_total, mass, entropy, cross = (pltpu.roll(total, lanes - k, 1) for k in (1, 2, 3, 4))
    div[...] = entropy / mass - jnp.log(mass) - cross / mass + top + jnp.log(exp_total)
    exp_scale = words / exp_total
    map_scale = words / mass

    @pl.loop(0, n)
    def _(source):
        here = lane == source * FIELDS
        row_top, row_exp, row_map = (
            jnp.sum(jnp.where(here, v, 0.0), axis=1, keepdims=True)
            for v in (top, exp_scale, map_scale)
        )

        @pl.loop(0, width // chunk)
        def _(c):
            at = pl.ds(pl.multiple_of(c * chunk, chunk), chunk)
            x = student[source, :, at].astype(jnp.float32)
            value = jnp.exp(x - row_top) * row_exp - mapped_of(source, at) * row_map
            grad[source, :, at] = value.astype(grad.dtype)


def body(teacher, student, block_maps, slot_index, slot_count):
    n = lax.axis_size("tok")
    rows = teacher.shape[1]
    half_rows, _, width = student.shape
    student_blocks, _, slots_all, depth, block = block_maps.shape
    span = teacher.shape[2] // n
    teacher_blocks = span // block
    lanes = max(LANES, n * FIELDS)
    used = jnp.arange(slots_all, dtype=jnp.int32)[None, :] < slot_count[:, :1]
    slots = jnp.where(used, slot_index[:, 0], teacher_blocks).reshape(-1)
    anywhere = pl.BlockSpec(memory_space=pl.ANY)
    in_vmem = pl.BlockSpec(memory_space=pltpu.VMEM)
    dma = pltpu.SemaphoreType.DMA
    grad, div = pl.pallas_call(
        functools.partial(kernel, n, float(n * width)),
        out_shape=(
            jax.ShapeDtypeStruct((n, half_rows, width), jnp.bfloat16),
            jax.ShapeDtypeStruct((half_rows, lanes), jnp.float32),
        ),
        in_specs=[anywhere, anywhere, anywhere, pl.BlockSpec(memory_space=pltpu.SMEM)],
        out_specs=(in_vmem, in_vmem),
        scratch_shapes=[
            pltpu.VMEM((n, rows, span), jnp.bfloat16),
            pltpu.VMEM((teacher_blocks + 1, rows, block), jnp.bfloat16),
            pltpu.VMEM((student_blocks, slots_all * depth, block), jnp.bfloat16),
            pltpu.VMEM((n, half_rows, width), jnp.bfloat16),
            pltpu.VMEM((n, rows, width), jnp.float32),
            pltpu.VMEM((n, half_rows, width), jnp.float32),
            pltpu.VMEM((half_rows, lanes), jnp.float32),
            pltpu.VMEM((n - 1, half_rows, lanes), jnp.float32),
            dma((3,)),
            dma((n - 1,)),
            dma((n - 1,)),
            dma((n,)),
            dma((n,)),
            dma((n - 1,)),
            dma((n - 1,)),
        ],
        compiler_params=pltpu.CompilerParams(
            collective_id=0, has_side_effects=True, vmem_limit_bytes=56 * 2**20
        ),
    )(
        teacher[0],
        jnp.swapaxes(student, 0, 1),
        block_maps.reshape(student_blocks, slots_all * depth, block),
        slots,
    )
    divergence = div.reshape(half_rows, -1, FIELDS)[:, :n, 0]
    return jnp.swapaxes(grad, 0, 1), divergence


def solution(mesh):
    return jax.shard_map(
        body,
        mesh=mesh,
        in_specs=(
            P(("groups", "tok"), None, "voc"),
            P("voc", "groups", "tok"),
            P("tok", "voc", None, None, None),
            P("tok", "voc", None),
            P("tok", "voc"),
        ),
        out_specs=(P("voc", "groups", "tok"), P("voc", "groups")),
        check_vma=False,
    )
```

```python
import functools

import jax
import jax.numpy as jnp
from jax import lax
from jax.experimental import pallas as pl
from jax.experimental.pallas import tpu as pltpu
from jax.sharding import PartitionSpec as P

MESH = pl.DeviceIdType.MESH
LANES = 128
FIELDS = 8
WINDOW = 4


def kernel(
    n, words, teacher, student_hbm, maps_hbm, slots, counts, grad, div,
    cols, work, maps, student, part, other_part, logits, mapped_all, scales, stats, gathered,
    local_sem, send_sem, recv_sem, half_send, half_recv, stat_send, stat_recv,
):
    rows = cols.shape[1]
    span = cols.shape[2]
    teacher_blocks = span // LANES
    student_blocks = maps.shape[0]
    slots_all = maps.shape[1] // LANES
    half_rows = student.shape[0]
    width = student.shape[2]
    lanes = stats.shape[1]
    chunk = 512
    me = lax.axis_index("tok")
    voc = lax.axis_index("voc")
    other = 1 - voc

    def partner(step):
        half = (step + 1) // 2
        odd = lax.rem(step, 2)
        mask = odd * half + (1 - odd) * (n - 1 - half)
        total, bit = 0, 1
        while bit < n:
            mine = lax.rem(me // bit, 2)
            flip = lax.rem(mask // bit, 2)
            total = total + bit * (mine + flip - 2 * mine * flip)
            bit *= 2
        return total

    def column_copy(step):
        target = partner(step)
        return pltpu.make_async_remote_copy(
            src_ref=teacher.at[:, pl.ds(pl.multiple_of(target * span, LANES), span)],
            dst_ref=cols.at[step + 1],
            send_sem=send_sem.at[step],
            recv_sem=recv_sem.at[step],
            device_id={"tok": target},
            device_id_type=MESH,
        )

    def half_copy(source):
        return pltpu.make_async_remote_copy(
            src_ref=part.at[source, pl.ds(pl.multiple_of(other * half_rows, 8), half_rows)],
            dst_ref=other_part.at[source],
            send_sem=half_send.at[source],
            recv_sem=half_recv.at[source],
            device_id={"voc": other},
            device_id_type=MESH,
        )

    def stat_copy(step):
        target = lax.rem(me + step + 1, n)
        return pltpu.make_async_remote_copy(
            src_ref=stats,
            dst_ref=gathered.at[step],
            send_sem=stat_send.at[step],
            recv_sem=stat_recv.at[step],
            device_id={"tok": target},
            device_id_type=MESH,
        )

    own_copy = pltpu.make_async_copy(
        teacher.at[:, pl.ds(pl.multiple_of(me * span, LANES), span)], cols.at[0], local_sem.at[0]
    )
    maps_copy = pltpu.make_async_copy(maps_hbm, maps, local_sem.at[1])
    student_copy = pltpu.make_async_copy(student_hbm, student, local_sem.at[2])
    own_copy.start()
    maps_copy.start()
    student_copy.start()

    barrier = pltpu.get_barrier_semaphore()

    @pl.loop(1, n)
    def _(step):
        pl.semaphore_signal(
            barrier, inc=1, device_id={"tok": lax.rem(me + step, n)}, device_id_type=MESH
        )

    pl.semaphore_signal(barrier, inc=1, device_id={"voc": other}, device_id_type=MESH)
    pl.semaphore_wait(barrier, n)

    for step in range(min(WINDOW, n - 1)):
        column_copy(step).start()

    work[teacher_blocks] = jnp.zeros((rows, LANES), work.dtype)
    stats[...] = jnp.zeros_like(stats)
    lane = lax.broadcasted_iota(jnp.int32, (half_rows, lanes), 1)

    def map_rows(slot, source):
        for block in range(teacher_blocks):
            work[block] = cols[slot, :, block * LANES : (block + 1) * LANES]

        @pl.loop(0, student_blocks, unroll=4)
        def _(block):
            picked = jnp.concatenate(
                [
                    work[lax.select(k < counts[block], slots[block, k], teacher_blocks)]
                    for k in range(slots_all)
                ],
                axis=1,
            )
            part[source, :, pl.ds(pl.multiple_of(block * LANES, LANES), LANES)] = jnp.dot(
                picked, maps[block], preferred_element_type=jnp.float32
            )

        half_copy(source).start()

    def mapped_of(source, at):
        mine = part[source, pl.ds(pl.multiple_of(voc * half_rows, 8), half_rows), at]
        return mine + other_part[source, :, at]

    def shard_rows(source):
        return pl.ds(source, half_rows, stride=n)

    def row_stats(source):
        def top_step(c, top):
            for k in range(chunk // LANES):
                top = jnp.maximum(top, logits[c * (chunk // LANES) + k, shard_rows(source), :])
            return top

        start = jnp.full((half_rows, LANES), -jnp.inf, jnp.float32)
        top = jnp.max(
            lax.fori_loop(0, width // chunk, top_step, start), axis=1, keepdims=True
        )
        half_copy(source).wait()

        def sum_step(c, sums):
            for k in range(chunk // LANES):
                block = c * (chunk // LANES) + k
                x = logits[block, shard_rows(source), :]
                mapped = mapped_of(source, pl.ds(pl.multiple_of(block * LANES, LANES), LANES))
                shifted = jnp.exp(x - top)
                logits[block, shard_rows(source), :] = shifted
                mapped_all[block, shard_rows(source), :] = mapped
                terms = (shifted, mapped, mapped * jnp.log(mapped), mapped * x)
                sums = tuple(s + v for s, v in zip(sums, terms))
            return sums

        zero = jnp.zeros((half_rows, LANES), jnp.float32)
        sums = lax.fori_loop(0, width // chunk, sum_step, (zero,) * 4)
        packed = stats[...]
        values = (top,) + tuple(jnp.sum(s, axis=1, keepdims=True) for s in sums)
        for field, value in enumerate(values):
            packed = jnp.where(lane == source * FIELDS + field, value, packed)
        stats[...] = packed

    own_copy.wait()
    maps_copy.wait()
    map_rows(0, me)
    student_copy.wait()

    @pl.loop(0, half_rows)
    def _(row):
        at = pl.ds(pl.multiple_of(row * n, 8), n)
        for c in range(width // LANES):
            logits[c, at, :] = student[row, :, c * LANES : (c + 1) * LANES].astype(jnp.float32)

    def source_of(step):
        return partner(step)

    @pl.loop(0, n - 1)
    def _(step):
        column_copy(step).wait()

        @pl.when(step + WINDOW < n - 1)
        def _():
            column_copy(step + WINDOW).start()

        map_rows(step + 1, source_of(step))
        row_stats(lax.select(step == 0, me, source_of(jnp.maximum(step - 1, 0))))

    row_stats(source_of(n - 2))

    @pl.loop(0, n - 1)
    def _(step):
        stat_copy(step).start()

    @pl.loop(0, n - 1)
    def _(step):
        stat_copy(step).wait()

    own = stats[...]
    top = lax.fori_loop(0, n - 1, lambda d, t: jnp.maximum(t, gathered[d]), own)
    is_exp = lax.rem(lane, FIELDS) == 1

    def scaled(g):
        return jnp.where(is_exp, g * jnp.exp(pltpu.roll(g - top, 1, 1)), g)

    total = lax.fori_loop(0, n - 1, lambda d, t: t + scaled(gathered[d]), scaled(own))
    exp_total, mass, entropy, cross = (pltpu.roll(total, lanes - k, 1) for k in (1, 2, 3, 4))
    div[...] = entropy / mass - jnp.log(mass) - cross / mass + top + jnp.log(exp_total)
    exp_scale = jnp.exp(own - top) * (words / exp_total)
    map_scale = words / mass

    @pl.loop(0, n)
    def _(source):
        here = lane == source * FIELDS
        for which, value in enumerate((exp_scale, map_scale)):
            column = jnp.sum(jnp.where(here, value, 0.0), axis=1, keepdims=True)
            scales[which, shard_rows(source), :] = jnp.broadcast_to(column, (half_rows, LANES))

    @pl.loop(0, half_rows)
    def _(row):
        at = pl.ds(pl.multiple_of(row * n, 8), n)
        row_exp, row_map = scales[0, at, :], scales[1, at, :]
        for c in range(width // LANES):
            value = logits[c, at, :] * row_exp - mapped_all[c, at, :] * row_map
            grad[row, :, c * LANES : (c + 1) * LANES] = value.astype(grad.dtype)


def body(teacher, student, block_maps, slot_index, slot_count):
    n = lax.axis_size("tok")
    rows = teacher.shape[1]
    half_rows, _, width = student.shape
    student_blocks, _, slots_all, depth, block = block_maps.shape
    span = teacher.shape[2] // n
    teacher_blocks = span // block
    lanes = max(LANES, n * FIELDS)
    anywhere = pl.BlockSpec(memory_space=pl.ANY)
    in_vmem = pl.BlockSpec(memory_space=pltpu.VMEM)
    dma = pltpu.SemaphoreType.DMA
    grad, div = pl.pallas_call(
        functools.partial(kernel, n, float(n * width)),
        out_shape=(
            jax.ShapeDtypeStruct((half_rows, n, width), jnp.bfloat16),
            jax.ShapeDtypeStruct((half_rows, lanes), jnp.float32),
        ),
        in_specs=[anywhere] * 3 + [pl.BlockSpec(memory_space=pltpu.SMEM)] * 2,
        out_specs=(in_vmem, in_vmem),
        scratch_shapes=[
            pltpu.VMEM((n, rows, span), jnp.bfloat16),
            pltpu.VMEM((teacher_blocks + 1, rows, block), jnp.bfloat16),
            pltpu.VMEM((student_blocks, slots_all * depth, block), jnp.bfloat16),
            pltpu.VMEM((half_rows, n, width), jnp.bfloat16),
            pltpu.VMEM((n, rows, width), jnp.float32),
            pltpu.VMEM((n, half_rows, width), jnp.float32),
            pltpu.VMEM((width // LANES, half_rows * n, LANES), jnp.float32),
            pltpu.VMEM((width // LANES, half_rows * n, LANES), jnp.float32),
            pltpu.VMEM((2, half_rows * n, LANES), jnp.float32),
            pltpu.VMEM((half_rows, lanes), jnp.float32),
            pltpu.VMEM((n - 1, half_rows, lanes), jnp.float32),
            dma((3,)),
            dma((n - 1,)),
            dma((n - 1,)),
            dma((n,)),
            dma((n,)),
            dma((n - 1,)),
            dma((n - 1,)),
        ],
        compiler_params=pltpu.CompilerParams(
            collective_id=0, has_side_effects=True, vmem_limit_bytes=60 * 2**20
        ),
    )(
        teacher[0],
        student,
        block_maps.reshape(student_blocks, slots_all * depth, block),
        slot_index[:, 0],
        slot_count[:, 0],
    )
    divergence = div.reshape(half_rows, -1, FIELDS)[:, :n, 0]
    return grad, divergence


def solution(mesh):
    return jax.shard_map(
        body,
        mesh=mesh,
        in_specs=(
            P(("groups", "tok"), None, "voc"),
            P("voc", "groups", "tok"),
            P("tok", "voc", None, None, None),
            P("tok", "voc", None),
            P("tok", "voc"),
        ),
        out_specs=(P("voc", "groups", "tok"), P("voc", "groups")),
        check_vma=False,
    )
```

```python
import functools

import jax
import jax.numpy as jnp
from jax import lax
from jax.experimental import pallas as pl
from jax.experimental.pallas import tpu as pltpu
from jax.sharding import PartitionSpec as P

MESH = pl.DeviceIdType.MESH
LANES = 128
FIELDS = 8
WINDOW = 7


def kernel(
    n, words, teacher, student_hbm, maps_hbm, slots, counts, grad, div,
    cols, work, maps, student, part, other_part, logits, mapped_all, scales, stats, gathered,
    local_sem, send_sem, recv_sem, half_send, half_recv, stat_send, stat_recv,
):
    rows = cols.shape[1]
    span = cols.shape[2]
    teacher_blocks = span // LANES
    student_blocks = maps.shape[0]
    slots_all = maps.shape[1] // LANES
    half_rows = student.shape[0]
    width = student.shape[2]
    lanes = stats.shape[1]
    chunk = 512
    me = lax.axis_index("tok")
    voc = lax.axis_index("voc")
    other = 1 - voc

    def partner(step):
        half = (step + 1) // 2
        odd = lax.rem(step, 2)
        mask = odd * half + (1 - odd) * (n - 1 - half)
        total, bit = 0, 1
        while bit < n:
            mine = lax.rem(me // bit, 2)
            flip = lax.rem(mask // bit, 2)
            total = total + bit * (mine + flip - 2 * mine * flip)
            bit *= 2
        return total

    def column_copy(step):
        target = partner(step)
        return pltpu.make_async_remote_copy(
            src_ref=teacher.at[:, pl.ds(pl.multiple_of(target * span, LANES), span)],
            dst_ref=cols.at[step + 1],
            send_sem=send_sem.at[step],
            recv_sem=recv_sem.at[step],
            device_id={"tok": target},
            device_id_type=MESH,
        )

    def half_copy(source):
        return pltpu.make_async_remote_copy(
            src_ref=part.at[source, pl.ds(pl.multiple_of(other * half_rows, 8), half_rows)],
            dst_ref=other_part.at[source],
            send_sem=half_send.at[source],
            recv_sem=half_recv.at[source],
            device_id={"voc": other},
            device_id_type=MESH,
        )

    def stat_copy(step):
        target = lax.rem(me + step + 1, n)
        return pltpu.make_async_remote_copy(
            src_ref=stats,
            dst_ref=gathered.at[step],
            send_sem=stat_send.at[step],
            recv_sem=stat_recv.at[step],
            device_id={"tok": target},
            device_id_type=MESH,
        )

    own_copy = pltpu.make_async_copy(
        teacher.at[:, pl.ds(pl.multiple_of(me * span, LANES), span)], cols.at[0], local_sem.at[0]
    )
    maps_copy = pltpu.make_async_copy(maps_hbm, maps, local_sem.at[1])
    student_copy = pltpu.make_async_copy(student_hbm, student, local_sem.at[2])
    own_copy.start()
    maps_copy.start()
    student_copy.start()

    barrier = pltpu.get_barrier_semaphore()

    @pl.loop(1, n)
    def _(step):
        pl.semaphore_signal(
            barrier, inc=1, device_id={"tok": lax.rem(me + step, n)}, device_id_type=MESH
        )

    pl.semaphore_signal(barrier, inc=1, device_id={"voc": other}, device_id_type=MESH)
    pl.semaphore_wait(barrier, n)

    for step in range(min(WINDOW, n - 1)):
        column_copy(step).start()

    work[teacher_blocks] = jnp.zeros((rows, LANES), work.dtype)
    stats[...] = jnp.zeros_like(stats)
    lane = lax.broadcasted_iota(jnp.int32, (half_rows, lanes), 1)

    def map_rows(slot, source):
        for block in range(teacher_blocks):
            work[block] = cols[slot, :, block * LANES : (block + 1) * LANES]

        @pl.loop(0, student_blocks, unroll=min(16, student_blocks))
        def _(block):
            picked = jnp.concatenate(
                [
                    work[lax.select(k < counts[block], slots[block, k], teacher_blocks)]
                    for k in range(slots_all)
                ],
                axis=1,
            )
            part[source, :, pl.ds(pl.multiple_of(block * LANES, LANES), LANES)] = jnp.dot(
                picked, maps[block], preferred_element_type=jnp.float32
            )

        half_copy(source).start()

    def mapped_of(source, at):
        mine = part[source, pl.ds(pl.multiple_of(voc * half_rows, 8), half_rows), at]
        return mine + other_part[source, :, at]

    def shard_rows(source):
        return pl.ds(source, half_rows, stride=n)

    def row_stats(source):
        def top_step(c, top):
            for k in range(chunk // LANES):
                top = jnp.maximum(top, logits[c * (chunk // LANES) + k, shard_rows(source), :])
            return top

        start = jnp.full((half_rows, LANES), -jnp.inf, jnp.float32)
        top = jnp.max(
            lax.fori_loop(0, width // chunk, top_step, start), axis=1, keepdims=True
        )
        half_copy(source).wait()

        def sum_step(c, sums):
            for k in range(chunk // LANES):
                block = c * (chunk // LANES) + k
                x = logits[block, shard_rows(source), :]
                mapped = mapped_of(source, pl.ds(pl.multiple_of(block * LANES, LANES), LANES))
                shifted = jnp.exp(x - top)
                logits[block, shard_rows(source), :] = shifted
                mapped_all[block, shard_rows(source), :] = mapped
                terms = (shifted, mapped, mapped * jnp.log(mapped), mapped * x)
                sums = tuple(s + v for s, v in zip(sums, terms))
            return sums

        zero = jnp.zeros((half_rows, LANES), jnp.float32)
        sums = lax.fori_loop(0, width // chunk, sum_step, (zero,) * 4)
        packed = stats[...]
        values = (top,) + tuple(jnp.sum(s, axis=1, keepdims=True) for s in sums)
        for field, value in enumerate(values):
            packed = jnp.where(lane == source * FIELDS + field, value, packed)
        stats[...] = packed

    own_copy.wait()
    maps_copy.wait()
    map_rows(0, me)
    student_copy.wait()

    @pl.loop(0, half_rows)
    def _(row):
        at = pl.ds(pl.multiple_of(row * n, 8), n)
        for c in range(width // LANES):
            logits[c, at, :] = student[row, :, c * LANES : (c + 1) * LANES].astype(jnp.float32)

    def source_of(step):
        return partner(step)

    @pl.loop(0, n - 1)
    def _(step):
        column_copy(step).wait()

        @pl.when(step + WINDOW < n - 1)
        def _():
            column_copy(step + WINDOW).start()

        map_rows(step + 1, source_of(step))
        row_stats(lax.select(step == 0, me, source_of(jnp.maximum(step - 1, 0))))

    row_stats(source_of(n - 2))

    @pl.loop(0, n - 1)
    def _(step):
        stat_copy(step).start()

    @pl.loop(0, n - 1)
    def _(step):
        stat_copy(step).wait()

    own = stats[...]
    top = lax.fori_loop(0, n - 1, lambda d, t: jnp.maximum(t, gathered[d]), own)
    is_exp = lax.rem(lane, FIELDS) == 1

    def scaled(g):
        return jnp.where(is_exp, g * jnp.exp(pltpu.roll(g - top, 1, 1)), g)

    total = lax.fori_loop(0, n - 1, lambda d, t: t + scaled(gathered[d]), scaled(own))
    exp_total, mass, entropy, cross = (pltpu.roll(total, lanes - k, 1) for k in (1, 2, 3, 4))
    spread = entropy / mass - jnp.log(mass) - cross / mass + top + jnp.log(exp_total)
    exp_scale = jnp.exp(own - top) * (words / exp_total)
    map_scale = words / mass

    div_lane = lax.broadcasted_iota(jnp.int32, (half_rows, n), 1)

    def unpack(source, tokens):
        here = lane == source * FIELDS
        for which, value in enumerate((exp_scale, map_scale)):
            column = jnp.sum(jnp.where(here, value, 0.0), axis=1, keepdims=True)
            scales[which, shard_rows(source), :] = jnp.broadcast_to(column, (half_rows, LANES))
        token = jnp.sum(jnp.where(here, spread, 0.0), axis=1, keepdims=True)
        return jnp.where(div_lane == source, token, tokens)

    div[...] = lax.fori_loop(0, n, unpack, jnp.zeros((half_rows, n), jnp.float32))

    @pl.loop(0, half_rows)
    def _(row):
        at = pl.ds(pl.multiple_of(row * n, 8), n)
        row_exp, row_map = scales[0, at, :], scales[1, at, :]
        for c in range(width // LANES):
            value = logits[c, at, :] * row_exp - mapped_all[c, at, :] * row_map
            grad[row, :, c * LANES : (c + 1) * LANES] = value.astype(grad.dtype)


def body(teacher, student, block_maps, slot_index, slot_count):
    n = lax.axis_size("tok")
    rows = teacher.shape[1]
    half_rows, _, width = student.shape
    student_blocks, _, slots_all, depth, block = block_maps.shape
    span = teacher.shape[2] // n
    teacher_blocks = span // block
    lanes = max(LANES, n * FIELDS)
    anywhere = pl.BlockSpec(memory_space=pl.ANY)
    in_vmem = pl.BlockSpec(memory_space=pltpu.VMEM)
    dma = pltpu.SemaphoreType.DMA
    grad, div = pl.pallas_call(
        functools.partial(kernel, n, float(n * width)),
        out_shape=(
            jax.ShapeDtypeStruct((half_rows, n, width), jnp.bfloat16),
            jax.ShapeDtypeStruct((half_rows, n), jnp.float32),
        ),
        in_specs=[anywhere] * 3 + [pl.BlockSpec(memory_space=pltpu.SMEM)] * 2,
        out_specs=(in_vmem, in_vmem),
        scratch_shapes=[
            pltpu.VMEM((n, rows, span), jnp.bfloat16),
            pltpu.VMEM((teacher_blocks + 1, rows, block), jnp.bfloat16),
            pltpu.VMEM((student_blocks, slots_all * depth, block), jnp.bfloat16),
            pltpu.VMEM((half_rows, n, width), jnp.bfloat16),
            pltpu.VMEM((n, rows, width), jnp.float32),
            pltpu.VMEM((n, half_rows, width), jnp.float32),
            pltpu.VMEM((width // LANES, half_rows * n, LANES), jnp.float32),
            pltpu.VMEM((width // LANES, half_rows * n, LANES), jnp.float32),
            pltpu.VMEM((2, half_rows * n, LANES), jnp.float32),
            pltpu.VMEM((half_rows, lanes), jnp.float32),
            pltpu.VMEM((n - 1, half_rows, lanes), jnp.float32),
            dma((3,)),
            dma((n - 1,)),
            dma((n - 1,)),
            dma((n,)),
            dma((n,)),
            dma((n - 1,)),
            dma((n - 1,)),
        ],
        compiler_params=pltpu.CompilerParams(
            collective_id=0, has_side_effects=True, vmem_limit_bytes=60 * 2**20
        ),
    )(
        teacher[0],
        student,
        block_maps.reshape(student_blocks, slots_all * depth, block),
        slot_index[:, 0],
        slot_count[:, 0],
    )
    return grad, div


def solution(mesh):
    return jax.shard_map(
        body,
        mesh=mesh,
        in_specs=(
            P(("groups", "tok"), None, "voc"),
            P("voc", "groups", "tok"),
            P("tok", "voc", None, None, None),
            P("tok", "voc", None),
            P("tok", "voc"),
        ),
        out_specs=(P("voc", "groups", "tok"), P("voc", "groups")),
        check_vma=False,
    )
```

```python
import functools

import jax
import jax.numpy as jnp
from jax import lax
from jax.experimental import pallas as pl
from jax.experimental.pallas import tpu as pltpu
from jax.sharding import PartitionSpec as P

MESH = pl.DeviceIdType.MESH
LANES = 128
FIELDS = 8
WINDOW = 7


def kernel(
    n, words, teacher, student_hbm, maps_hbm, slots, counts, grad, div,
    cols, work, maps, student, part, other_part, logits, mapped_all, scales, stats, gathered,
    local_sem, send_sem, recv_sem, half_send, half_recv, stat_send, stat_recv,
):
    rows = cols.shape[1]
    span = cols.shape[2]
    teacher_blocks = span // LANES
    student_blocks = maps.shape[0]
    slots_all = maps.shape[1] // LANES
    half_rows = student.shape[0]
    width = student.shape[2]
    lanes = stats.shape[1]
    chunk = 1024
    me = lax.axis_index("tok")
    voc = lax.axis_index("voc")
    other = 1 - voc

    def partner(step):
        half = (step + 1) // 2
        odd = lax.rem(step, 2)
        mask = odd * half + (1 - odd) * (n - 1 - half)
        total, bit = 0, 1
        while bit < n:
            mine = lax.rem(me // bit, 2)
            flip = lax.rem(mask // bit, 2)
            total = total + bit * (mine + flip - 2 * mine * flip)
            bit *= 2
        return total

    def column_copy(step):
        target = partner(step)
        return pltpu.make_async_remote_copy(
            src_ref=teacher.at[:, pl.ds(pl.multiple_of(target * span, LANES), span)],
            dst_ref=cols.at[step + 1],
            send_sem=send_sem.at[step],
            recv_sem=recv_sem.at[step],
            device_id={"tok": target},
            device_id_type=MESH,
        )

    def half_copy(source):
        return pltpu.make_async_remote_copy(
            src_ref=part.at[source, pl.ds(pl.multiple_of(other * half_rows, 8), half_rows)],
            dst_ref=other_part.at[source],
            send_sem=half_send.at[source],
            recv_sem=half_recv.at[source],
            device_id={"voc": other},
            device_id_type=MESH,
        )

    def stat_copy(step):
        target = lax.rem(me + step + 1, n)
        return pltpu.make_async_remote_copy(
            src_ref=stats,
            dst_ref=gathered.at[step],
            send_sem=stat_send.at[step],
            recv_sem=stat_recv.at[step],
            device_id={"tok": target},
            device_id_type=MESH,
        )

    own_copy = pltpu.make_async_copy(
        teacher.at[:, pl.ds(pl.multiple_of(me * span, LANES), span)], cols.at[0], local_sem.at[0]
    )
    maps_copy = pltpu.make_async_copy(maps_hbm, maps, local_sem.at[1])
    student_copy = pltpu.make_async_copy(student_hbm, student, local_sem.at[2])
    own_copy.start()
    maps_copy.start()
    student_copy.start()

    barrier = pltpu.get_barrier_semaphore()

    @pl.loop(1, n)
    def _(step):
        pl.semaphore_signal(
            barrier, inc=1, device_id={"tok": lax.rem(me + step, n)}, device_id_type=MESH
        )

    pl.semaphore_signal(barrier, inc=1, device_id={"voc": other}, device_id_type=MESH)
    pl.semaphore_wait(barrier, n)

    for step in range(min(WINDOW, n - 1)):
        column_copy(step).start()

    work[teacher_blocks] = jnp.zeros((rows, LANES), work.dtype)
    stats[...] = jnp.zeros_like(stats)
    lane = lax.broadcasted_iota(jnp.int32, (half_rows, lanes), 1)

    def map_rows(slot, source):
        for block in range(teacher_blocks):
            work[block] = cols[slot, :, block * LANES : (block + 1) * LANES]

        @pl.loop(0, student_blocks, unroll=min(16, student_blocks))
        def _(block):
            picked = jnp.concatenate(
                [
                    work[lax.select(k < counts[block], slots[block, k], teacher_blocks)]
                    for k in range(slots_all)
                ],
                axis=1,
            )
            part[source, :, pl.ds(pl.multiple_of(block * LANES, LANES), LANES)] = jnp.dot(
                picked, maps[block], preferred_element_type=jnp.float32
            )

        half_copy(source).start()

    def mapped_of(source, at):
        mine = part[source, pl.ds(pl.multiple_of(voc * half_rows, 8), half_rows), at]
        return mine + other_part[source, :, at]

    def shard_rows(source):
        return pl.ds(source, half_rows, stride=n)

    def row_stats(source):
        def top_step(c, top):
            for k in range(chunk // LANES):
                top = jnp.maximum(top, logits[c * (chunk // LANES) + k, shard_rows(source), :])
            return top

        start = jnp.full((half_rows, LANES), -jnp.inf, jnp.float32)
        top = jnp.max(
            lax.fori_loop(0, width // chunk, top_step, start), axis=1, keepdims=True
        )
        half_copy(source).wait()

        def sum_step(c, sums):
            for k in range(chunk // LANES):
                block = c * (chunk // LANES) + k
                x = logits[block, shard_rows(source), :]
                mapped = mapped_of(source, pl.ds(pl.multiple_of(block * LANES, LANES), LANES))
                shifted = jnp.exp(x - top)
                logits[block, shard_rows(source), :] = shifted
                mapped_all[block, shard_rows(source), :] = mapped
                terms = (shifted, mapped, mapped * jnp.log(mapped), mapped * x)
                sums = tuple(s + v for s, v in zip(sums, terms))
            return sums

        zero = jnp.zeros((half_rows, LANES), jnp.float32)
        sums = lax.fori_loop(0, width // chunk, sum_step, (zero,) * 4)
        packed = stats[...]
        values = (top,) + tuple(jnp.sum(s, axis=1, keepdims=True) for s in sums)
        for field, value in enumerate(values):
            packed = jnp.where(lane == source * FIELDS + field, value, packed)
        stats[...] = packed

    own_copy.wait()
    maps_copy.wait()
    map_rows(0, me)
    student_copy.wait()

    @pl.loop(0, half_rows)
    def _(row):
        at = pl.ds(pl.multiple_of(row * n, 8), n)
        for c in range(width // LANES):
            logits[c, at, :] = student[row, :, c * LANES : (c + 1) * LANES].astype(jnp.float32)

    def source_of(step):
        return partner(step)

    @pl.loop(0, n - 1)
    def _(step):
        column_copy(step).wait()

        @pl.when(step + WINDOW < n - 1)
        def _():
            column_copy(step + WINDOW).start()

        map_rows(step + 1, source_of(step))
        row_stats(lax.select(step == 0, me, source_of(jnp.maximum(step - 1, 0))))

    row_stats(source_of(n - 2))

    @pl.loop(0, n - 1)
    def _(step):
        stat_copy(step).start()

    @pl.loop(0, n - 1)
    def _(step):
        stat_copy(step).wait()

    own = stats[...]
    top = lax.fori_loop(0, n - 1, lambda d, t: jnp.maximum(t, gathered[d]), own)
    is_exp = lax.rem(lane, FIELDS) == 1

    def scaled(g):
        return jnp.where(is_exp, g * jnp.exp(pltpu.roll(g - top, 1, 1)), g)

    total = lax.fori_loop(0, n - 1, lambda d, t: t + scaled(gathered[d]), scaled(own))
    exp_total, mass, entropy, cross = (pltpu.roll(total, lanes - k, 1) for k in (1, 2, 3, 4))
    spread = entropy / mass - jnp.log(mass) - cross / mass + top + jnp.log(exp_total)
    exp_scale = jnp.exp(own - top) * (words / exp_total)
    map_scale = words / mass

    div_lane = lax.broadcasted_iota(jnp.int32, (half_rows, n), 1)

    def unpack(source, tokens):
        here = lane == source * FIELDS
        for which, value in enumerate((exp_scale, map_scale)):
            column = jnp.sum(jnp.where(here, value, 0.0), axis=1, keepdims=True)
            scales[which, shard_rows(source), :] = jnp.broadcast_to(column, (half_rows, LANES))
        token = jnp.sum(jnp.where(here, spread, 0.0), axis=1, keepdims=True)
        return jnp.where(div_lane == source, token, tokens)

    div[...] = lax.fori_loop(0, n, unpack, jnp.zeros((half_rows, n), jnp.float32))

    @pl.loop(0, half_rows)
    def _(row):
        at = pl.ds(pl.multiple_of(row * n, 8), n)
        row_exp, row_map = scales[0, at, :], scales[1, at, :]
        for c in range(width // LANES):
            value = logits[c, at, :] * row_exp - mapped_all[c, at, :] * row_map
            grad[row, :, c * LANES : (c + 1) * LANES] = value.astype(grad.dtype)


def body(teacher, student, block_maps, slot_index, slot_count):
    n = lax.axis_size("tok")
    rows = teacher.shape[1]
    half_rows, _, width = student.shape
    student_blocks, _, slots_all, depth, block = block_maps.shape
    span = teacher.shape[2] // n
    teacher_blocks = span // block
    lanes = max(LANES, n * FIELDS)
    anywhere = pl.BlockSpec(memory_space=pl.ANY)
    in_vmem = pl.BlockSpec(memory_space=pltpu.VMEM)
    dma = pltpu.SemaphoreType.DMA
    grad, div = pl.pallas_call(
        functools.partial(kernel, n, float(n * width)),
        out_shape=(
            jax.ShapeDtypeStruct((half_rows, n, width), jnp.bfloat16),
            jax.ShapeDtypeStruct((half_rows, n), jnp.float32),
        ),
        in_specs=[anywhere] * 3 + [pl.BlockSpec(memory_space=pltpu.SMEM)] * 2,
        out_specs=(in_vmem, in_vmem),
        scratch_shapes=[
            pltpu.VMEM((n, rows, span), jnp.bfloat16),
            pltpu.VMEM((teacher_blocks + 1, rows, block), jnp.bfloat16),
            pltpu.VMEM((student_blocks, slots_all * depth, block), jnp.bfloat16),
            pltpu.VMEM((half_rows, n, width), jnp.bfloat16),
            pltpu.VMEM((n, rows, width), jnp.float32),
            pltpu.VMEM((n, half_rows, width), jnp.float32),
            pltpu.VMEM((width // LANES, half_rows * n, LANES), jnp.float32),
            pltpu.VMEM((width // LANES, half_rows * n, LANES), jnp.float32),
            pltpu.VMEM((2, half_rows * n, LANES), jnp.float32),
            pltpu.VMEM((half_rows, lanes), jnp.float32),
            pltpu.VMEM((n - 1, half_rows, lanes), jnp.float32),
            dma((3,)),
            dma((n - 1,)),
            dma((n - 1,)),
            dma((n,)),
            dma((n,)),
            dma((n - 1,)),
            dma((n - 1,)),
        ],
        compiler_params=pltpu.CompilerParams(
            collective_id=0, has_side_effects=True, vmem_limit_bytes=60 * 2**20
        ),
    )(
        teacher[0],
        student,
        block_maps.reshape(student_blocks, slots_all * depth, block),
        slot_index[:, 0],
        slot_count[:, 0],
    )
    return grad, div


def solution(mesh):
    return jax.shard_map(
        body,
        mesh=mesh,
        in_specs=(
            P(("groups", "tok"), None, "voc"),
            P("voc", "groups", "tok"),
            P("tok", "voc", None, None, None),
            P("tok", "voc", None),
            P("tok", "voc"),
        ),
        out_specs=(P("voc", "groups", "tok"), P("voc", "groups")),
        check_vma=False,
    )
```
